256 devices in a mesh: row: 8 (over z), col: 4 (over y_lo, core), depth: 8 (over y_hi, x).
Axes of the slice: x: 4, y: 4 (y_hi: 2, y_lo: 2; y = y_hi * 2 + y_lo), z: 8, core: 2. Of those that a mesh axis runs over, the one named last changes fastest.
Arguments:
- tokens: bfloat16 [1536, 12288], P(('row', 'col'), 'depth'), may hold values from -6 to 6
- up_weight: bfloat16 [12288, 24576], P('depth', ('row', 'col')), may hold values from -0.0546875 to 0.0546875
- up_bias: float32 [24576], P(('row', 'col')), may hold values from -3 to 3
- down_weight: bfloat16 [24576, 12288], P(('row', 'col'), 'depth'), may hold values from -0.0390625 to 0.0390625
- down_bias: float32 [12288], P('depth'), may hold values from -3 to 3
Outputs:
- layer_out: bfloat16 [1536, 12288], P(('row', 'col'), 'depth')
The draws below stay inside these ranges and needn't reach their ends.
All inputs are finite; a program needn't handle non-finite values.
Results may differ from the reference program's by a relative error of at most 0.0043.
Values may be sent and summed in bfloat16 or wider, within the bound.
A program may use at most 64 MiB of HBM per device.

```python
import jax
import jax.numpy as jnp
from jax import lax

D = 12288
F = 24576
TOKENS = 1536
N_ROW = 8
N_COL = 4


def shard_levels(stream_key, shape, split, low, high):
    factor_of = 1.0
    for dim, parts in split:
        draws = jax.random.uniform(jax.random.fold_in(jax.random.fold_in(stream_key, 6), dim), (parts,), jnp.float32, low / len(split), high / len(split))
        factor_of = factor_of * jnp.repeat(jnp.exp(draws), shape[dim] // parts).reshape((-1,) + (1,) * (len(shape) - 1 - dim))
    return factor_of


def scatter_about(rng, extent, scale, bound, shards=(), held_as=jnp.bfloat16):
    array = scale * jax.random.normal(rng, extent, jnp.float32)
    if shards:
        array = array * shard_levels(rng, extent, shards, -0.22, 0.18)
    return jnp.clip(array, -bound, bound).astype(held_as)


def setup_inputs(seed: int = 0) -> dict:
    keys = jax.random.split(jax.random.key(seed), 6)
    return {
        "tokens": scatter_about(keys[0], (TOKENS, D), 1.0, 6.0, ((0, 32), (1, 8))),
        "up_weight": scatter_about(keys[1], (D, F), D ** -0.5, 0.0546875, ((0, 8), (1, 32))),
        "up_bias": scatter_about(keys[2], (F,), 0.5, 3.0, ((0, 32),), jnp.float32),
        "down_weight": scatter_about(keys[3], (F, D), F ** -0.5, 0.0390625, ((0, 32), (1, 8))),
        "down_bias": scatter_about(keys[4], (D,), 0.5, 3.0, ((0, 8),), jnp.float32),
    }


def reference(tokens, up_weight, up_bias, down_weight, down_bias):
    pre_act = jnp.dot(tokens, up_weight, preferred_element_type=jnp.float32) + up_bias
    activated = jax.nn.gelu(pre_act, approximate=True).astype(jnp.bfloat16)
    groups = N_ROW * N_COL
    width = F // groups
    act_blocks = activated.reshape(TOKENS, groups, width).transpose(1, 0, 2)
    weight_blocks = down_weight.reshape(groups, width, D)

    def add_block(summed, pair):
        act_part, weight_part = pair
        term = jnp.dot(act_part, weight_part, preferred_element_type=jnp.float32)
        return summed + term, None

    summed, _ = lax.scan(add_block, jnp.zeros((TOKENS, D), jnp.float32), (act_blocks, weight_blocks))
    return (summed + down_bias).astype(jnp.bfloat16)
```

```python
import jax
import jax.numpy as jnp
from jax import lax
from jax.experimental import pallas as pl
from jax.experimental.pallas import tpu as pltpu
from jax.sharding import PartitionSpec as P

NC = 3
RB = 16
NZ = 8
ORDER = (
    (0, 1, 0), (0, 2, 0), (0, 0, 0), (0, 1, 1), (0, 2, 1), (1, 2, 0), (1, 1, 0), (0, 1, 2), (0, 2, 2),
    (1, 1, 1), (0, 1, 3), (1, 2, 1), (2, 2, 0), (0, 2, 3), (1, 1, 2), (2, 1, 0), (0, 0, 1), (1, 2, 2),
    (3, 2, 0), (0, 1, 4), (0, 2, 4), (1, 0, 0), (1, 1, 3), (2, 1, 2), (0, 1, 5), (0, 0, 2), (1, 2, 3),
    (2, 2, 2), (0, 2, 5), (1, 2, 4), (0, 0, 3), (2, 1, 3), (1, 1, 4), (1, 0, 1), (2, 2, 4), (0, 0, 4),
    (3, 1, 2), (2, 1, 4), (2, 2, 3), (4, 2, 0), (1, 0, 3), (2, 1, 1), (0, 0, 5), (3, 2, 4), (3, 1, 4),
    (1, 0, 4), (1, 0, 2), (2, 0, 3), (3, 2, 3), (3, 1, 3), (4, 2, 4), (4, 1, 4), (2, 0, 4), (2, 2, 1),
    (5, 2, 4), (4, 1, 2), (2, 0, 2), (5, 1, 4), (3, 0, 4), (3, 2, 2), (3, 0, 3), (2, 0, 0), (4, 2, 3),
    (2, 0, 1), (3, 2, 1), (4, 1, 3), (5, 2, 3), (3, 0, 2), (4, 0, 4), (5, 1, 3), (4, 2, 2), (3, 1, 0),
    (5, 0, 4), (4, 0, 3), (5, 2, 2), (3, 0, 1), (4, 2, 1), (5, 0, 3), (4, 0, 2), (5, 2, 1), (3, 1, 1),
    (4, 1, 0), (5, 0, 2), (4, 0, 1), (3, 0, 0), (5, 1, 2), (4, 1, 1), (5, 0, 1), (4, 0, 0), (5, 2, 0),
    (5, 1, 1), (5, 0, 0), (5, 1, 0), (6, 0, 0), (6, 2, 0), (6, 1, 0),
)
CORE = jnp.float32
MESH = pl.DeviceIdType.MESH
GROUPS = ((0, 1), (1, 2), (3, 2), (5, 2), (7, 1))


def kernel(
    tok, w1_hbm, b1, w2_hbm, b2, out,
    G, W1, W2, XF, XS, XR, YS, YR, A, OF, CS, CR, ZS, ZR, FS, LS, LR,
    load_sem, ss, rs,
):
    z = lax.axis_index("row")
    col = lax.axis_index("col")
    dep = lax.axis_index("depth")
    yl, c = col // 2, col % 2
    yh, x = dep // 4, dep % 4

    up_z = ((z + 1) % NZ, col, dep)
    dn_z = ((z + NZ - 1) % NZ, col, dep)
    mate = (z, yl * 2 + (1 - c), dep)
    near_y = (z, (1 - yl) * 2 + c, dep)
    far_y = (z, col, (1 - yh) * 4 + x)
    xs = [(x + d) % 4 for d in (1, 2, 3)]
    x_dev = [(z, col, yh * 4 + xd) for xd in xs]

    loads = [
        pltpu.make_async_copy(tok.at[pl.ds(k * RB, RB)], G.at[k, 0, c, yl], load_sem.at[k])
        for k in range(NC)
    ]
    loads.append(pltpu.make_async_copy(w1_hbm, W1, load_sem.at[NC]))
    loads.append(pltpu.make_async_copy(w2_hbm, W2, load_sem.at[NC + 1]))
    for copy in loads:
        copy.start()

    barrier = pltpu.get_barrier_semaphore()
    peers = [up_z, dn_z, mate, near_y, far_y] + x_dev
    for dev in peers:
        pl.semaphore_signal(barrier, inc=1, device_id=dev, device_id_type=MESH)
    pl.semaphore_wait(barrier, len(peers))

    copies = {}
    waited = set()

    def send(name, src, dst, dev):
        i = len(copies)
        copy = pltpu.make_async_remote_copy(
            src_ref=src, dst_ref=dst, send_sem=ss.at[i], recv_sem=rs.at[i],
            device_id=dev, device_id_type=MESH,
        )
        copy.start()
        copies[name] = copy

    def arrived(*name):
        copies[name].wait_recv()

    def to_mate(k, g):
        s, n = GROUPS[g]
        part = G.at[k, pl.ds(s, n), c]
        send(("mate", k, g), part, part, mate)

    def gather(k, step):
        if step == 0:
            loads[k].wait()
            own = G.at[k, 0, c, yl]
            send(("near", k), own, own, near_y)
        elif step == 1:
            arrived("near", k)
            send(("up", k, 1), G.at[k, 0, c], G.at[k, 1, c], up_z)
            send(("dn", k, 1), G.at[k, 0, c], G.at[k, 2, c], dn_z)
            to_mate(k, 0)
        elif step < 4:
            arrived("up", k, step - 1)
            s = 2 * step - 3
            send(("up", k, step), G.at[k, s, c], G.at[k, s + 2, c], up_z)
            arrived("dn", k, step - 1)
            send(("dn", k, step), G.at[k, s + 1, c], G.at[k, s + 3, c], dn_z)
            to_mate(k, step - 1)
        elif step == 4:
            arrived("up", k, 3)
            send(("up", k, 4), G.at[k, 5, c, 0], G.at[k, 7, c, 0], up_z)
            arrived("dn", k, 3)
            send(("dn", k, 4), G.at[k, 6, c, 1], G.at[k, 7, c, 1], dn_z)
            to_mate(k, 3)
        else:
            arrived("up", k, 4)
            arrived("dn", k, 4)
            to_mate(k, 4)

    def up_proj(k, g):
        s, n = GROUPS[g]
        if NC not in waited:
            waited.add(NC)
            loads[NC].wait()
        arrived("mate", k, g)

        @pl.loop(0, 3)
        def _(t):
            cols = pl.ds(pl.multiple_of(t * 256, 256), 256)
            lhs = G[k, pl.ds(s, n)].reshape(n * 4 * RB, 1536)
            r = jnp.dot(lhs, W1[:, cols], preferred_element_type=jnp.float32)
            r = r.reshape(n, 4, RB, 256)
            for i in range(n):
                for j in range(4):
                    XF[k, j, s + i, :, cols] = r[i, j]
                    XS[k, j, s + i, :, cols] = r[i, j].astype(jnp.bfloat16)

        for d in (1, 0, 2):
            send(("xs", k, g, d), XS.at[k, xs[d], pl.ds(s, n)], XR.at[k, d, pl.ds(s, n)], x_dev[d])

    def x_sum(k, g):
        s, n = GROUPS[g]
        for d in range(3):
            arrived("xs", k, g, d)
        rows = pl.ds(s, n)
        total = XF[k, x, rows]
        for d in range(3):
            total = total + XR[k, d, rows].astype(jnp.float32)
        YS[k, rows] = total
        send(("far", k, g), YS.at[k, rows], YR.at[k, rows], far_y)

    def activate(k, g):
        s, n = GROUPS[g]
        arrived("far", k, g)
        rows = pl.ds(s, n)
        v = YS[k, rows] + YR[k, rows] + b1[...].reshape(1, 1, 768)
        A[k, x, rows] = jax.nn.gelu(v, approximate=True).astype(jnp.bfloat16)
        for d in (1, 0, 2):
            send(("act", k, g, d), A.at[k, x, rows], A.at[k, x, rows], x_dev[d])

    def down_proj(k, g):
        s, n = GROUPS[g]
        if NC + 1 not in waited:
            waited.add(NC + 1)
            loads[NC + 1].wait()
        for d in range(3):
            arrived("act", k, g, d)
        first = c == 0

        @pl.loop(0, 6)
        def _(t):
            cols = pl.ds(pl.multiple_of(t * 256, 256), 256)
            lhs = A[k, :, pl.ds(s, n)].reshape(4 * n * RB, 768)
            r = jnp.dot(lhs, W2[:, cols], preferred_element_type=jnp.float32)
            r = r.reshape(2, 2, n, RB, 256)
            mine = jnp.where(first, r[0], r[1])
            other = jnp.where(first, r[1], r[0]).astype(CORE)
            for i in range(n):
                for j in range(2):
                    OF[k, s + i, j, :, cols] = mine[j, i]
                    CS[k, s + i, j, :, cols] = other[j, i]

        send(("core", k, g), CS.at[k, pl.ds(s, n)], CR.at[k, pl.ds(s, n)], mate)

    def reduce_z(k, g):
        s, n = GROUPS[g]
        arrived("core", k, g)

        def term(slot, block):
            return OF[k, slot, block] + CR[k, slot, block].astype(jnp.float32)

        if g == 4:
            for b in range(2):
                ZS[k, 7, b] = term(7, b).astype(jnp.bfloat16)
            send(("zdn", k, 4), ZS.at[k, 7, 0], ZR.at[k, 5, 0], dn_z)
            send(("zup", k, 4), ZS.at[k, 7, 1], ZR.at[k, 6, 1], up_z)
        elif g > 0:
            for name, slot, dev, there in (("zdn", s, dn_z, (s - 2) if g > 1 else 0), ("zup", s + 1, up_z, (s - 1) if g > 1 else 7)):
                arrived(name, k, g + 1)
                for b in range(2):
                    v = term(slot, b)
                    if g < 3 or b == (0 if name == "zdn" else 1):
                        v = v + ZR[k, slot, b].astype(jnp.float32)
                    ZS[k, slot, b] = v.astype(jnp.bfloat16)
                send((name, k, g), ZS.at[k, slot], ZR.at[k, there], dev)
        else:
            arrived("zdn", k, 1)
            arrived("zup", k, 1)
            for b in range(2):
                FS[k, b] = term(0, b) + ZR[k, 0, b].astype(jnp.float32) + ZR[k, 7, b].astype(jnp.float32)
            LS[k] = FS[k, 1 - yl]
            send(("last", k), LS.at[k], LR.at[k], near_y)

    def finish(k):
        arrived("last", k)
        v = FS[k, yl] + LR[k] + b2[...]
        out[pl.ds(k * RB, RB)] = v.astype(jnp.bfloat16)

    what = (gather, up_proj, x_sum, activate, down_proj, reduce_z, finish)
    for w, k, i in ORDER:
        what[w](*((k,) if w == 6 else (k, i)))

    for copy in copies.values():
        copy.wait_send()


def per_device(tokens, up_weight, up_bias, down_weight, down_bias):
    f32, bf16 = jnp.float32, jnp.bfloat16
    any_spec = pl.BlockSpec(memory_space=pl.ANY)
    vmem = pl.BlockSpec(memory_space=pltpu.VMEM)
    n_copies = NC * 64
    return pl.pallas_call(
        kernel,
        out_shape=jax.ShapeDtypeStruct((48, 1536), bf16),
        in_specs=[any_spec, any_spec, vmem, any_spec, vmem],
        out_specs=vmem,
        scratch_shapes=[
            pltpu.VMEM((NC, NZ, 2, 2, RB, 1536), bf16),
            pltpu.VMEM((1536, 768), bf16),
            pltpu.VMEM((768, 1536), bf16),
            pltpu.VMEM((NC, 4, NZ, RB, 768), f32),
            pltpu.VMEM((NC, 4, NZ, RB, 768), bf16),
            pltpu.VMEM((NC, 3, NZ, RB, 768), bf16),
            pltpu.VMEM((NC, NZ, RB, 768), f32),
            pltpu.VMEM((NC, NZ, RB, 768), f32),
            pltpu.VMEM((NC, 4, NZ, RB, 768), bf16),
            pltpu.VMEM((NC, NZ, 2, RB, 1536), f32),
            pltpu.VMEM((NC, NZ, 2, RB, 1536), CORE),
            pltpu.VMEM((NC, NZ, 2, RB, 1536), CORE),
            pltpu.VMEM((NC, NZ, 2, RB, 1536), bf16),
            pltpu.VMEM((NC, NZ, 2, RB, 1536), bf16),
            pltpu.VMEM((NC, 2, RB, 1536), f32),
            pltpu.VMEM((NC, RB, 1536), f32),
            pltpu.VMEM((NC, RB, 1536), f32),
            pltpu.SemaphoreType.DMA((NC + 2,)),
            pltpu.SemaphoreType.DMA((n_copies,)),
            pltpu.SemaphoreType.DMA((n_copies,)),
        ],
        compiler_params=pltpu.CompilerParams(
            collective_id=0, has_side_effects=True, vmem_limit_bytes=56 * 2**20
        ),
        cost_estimate=pl.CostEstimate(flops=7_300_000_000, bytes_accessed=5_000_000, transcendentals=600_000),
    )(tokens, up_weight, up_bias.reshape(1, 768), down_weight, down_bias.reshape(1, 1536))


def solution(mesh):
    return jax.shard_map(
        per_device,
        mesh=mesh,
        in_specs=(
            P(("row", "col"), "depth"),
            P("depth", ("row", "col")),
            P(("row", "col")),
            P(("row", "col"), "depth"),
            P("depth"),
        ),
        out_specs=P(("row", "col"), "depth"),
        check_vma=False,
    )
```

```python
import jax
import jax.numpy as jnp
from jax import lax
from jax.experimental import pallas as pl
from jax.experimental.pallas import tpu as pltpu
from jax.sharding import PartitionSpec as P

NC = 3
RB = 16
NZ = 8
ORDER = (
    (0, 0, 0), (0, 2, 0), (0, 1, 0), (0, 0, 1), (1, 0, 0), (0, 2, 1), (0, 0, 2), (1, 2, 0), (0, 2, 2),
    (1, 0, 1), (0, 1, 1), (1, 2, 1), (0, 0, 3), (1, 1, 0), (1, 0, 2), (2, 0, 0), (0, 2, 3), (1, 2, 2),
    (0, 1, 2), (2, 0, 1), (0, 0, 4), (3, 0, 0), (2, 1, 0), (2, 2, 1), (0, 2, 4), (1, 0, 3), (0, 1, 3),
    (1, 1, 1), (0, 0, 5), (0, 2, 5), (2, 2, 2), (1, 0, 4), (2, 2, 0), (1, 2, 4), (0, 1, 4), (1, 2, 3),
    (2, 0, 3), (1, 1, 3), (0, 1, 5), (2, 2, 4), (2, 0, 4), (1, 1, 4), (2, 2, 3), (3, 0, 3), (3, 2, 4),
    (4, 0, 0), (3, 0, 4), (2, 1, 4), (2, 1, 3), (1, 1, 2), (2, 0, 2), (4, 0, 3), (3, 1, 4), (3, 2, 3),
    (4, 0, 4), (4, 2, 4), (3, 1, 3), (5, 0, 4), (2, 1, 2), (2, 1, 1), (4, 1, 4), (3, 0, 2), (5, 2, 4),
    (3, 2, 2), (5, 1, 4), (4, 2, 3), (5, 0, 3), (3, 1, 2), (4, 1, 3), (5, 2, 3), (3, 0, 1), (4, 0, 2),
    (3, 2, 1), (5, 1, 3), (4, 2, 2), (5, 0, 2), (3, 1, 1), (4, 1, 2), (5, 2, 2), (4, 0, 1), (5, 1, 2),
    (3, 2, 0), (4, 2, 1), (5, 0, 1), (4, 1, 1), (5, 2, 1), (3, 1, 0), (4, 2, 0), (5, 1, 1), (5, 0, 0),
    (4, 1, 0), (5, 2, 0), (5, 1, 0), (6, 0, 0), (6, 2, 0), (6, 1, 0),
)
CORE = jnp.float32
MESH = pl.DeviceIdType.MESH
GROUPS = ((0, 1), (1, 2), (3, 2), (5, 2), (7, 1))


def kernel(
    tok, w1_hbm, b1, w2_hbm, b2, out,
    G, W1, W2, XF, XS, XR, YS, YR, A, OF, CS, CR, ZS, ZR, FS, LS, LR,
    load_sem, ss, rs,
):
    z = lax.axis_index("row")
    col = lax.axis_index("col")
    dep = lax.axis_index("depth")
    yl, c = col // 2, col % 2
    yh, x = dep // 4, dep % 4

    up_z = ((z + 1) % NZ, col, dep)
    dn_z = ((z + NZ - 1) % NZ, col, dep)
    mate = (z, yl * 2 + (1 - c), dep)
    near_y = (z, (1 - yl) * 2 + c, dep)
    far_y = (z, col, (1 - yh) * 4 + x)
    xs = [(x + d) % 4 for d in (1, 2, 3)]
    x_dev = [(z, col, yh * 4 + xd) for xd in xs]

    loads = [
        pltpu.make_async_copy(tok.at[pl.ds(k * RB, RB)], G.at[k, 0, c, yl], load_sem.at[k])
        for k in range(NC)
    ]
    loads.append(pltpu.make_async_copy(w1_hbm, W1, load_sem.at[NC]))
    loads.append(pltpu.make_async_copy(w2_hbm, W2, load_sem.at[NC + 1]))
    for copy in loads:
        copy.start()

    barrier = pltpu.get_barrier_semaphore()
    peers = [up_z, dn_z, mate, near_y, far_y] + x_dev
    for dev in peers:
        pl.semaphore_signal(barrier, inc=1, device_id=dev, device_id_type=MESH)
    pl.semaphore_wait(barrier, len(peers))

    copies = {}
    waited = set()

    def send(name, src, dst, dev):
        i = len(copies)
        copy = pltpu.make_async_remote_copy(
            src_ref=src, dst_ref=dst, send_sem=ss.at[i], recv_sem=rs.at[i],
            device_id=dev, device_id_type=MESH,
        )
        copy.start()
        copies[name] = copy

    def arrived(*name):
        copies[name].wait_recv()

    def to_mate(k, g):
        s, n = GROUPS[g]
        part = G.at[k, pl.ds(s, n), c]
        send(("mate", k, g), part, part, mate)

    def gather(k, step):
        if step == 0:
            loads[k].wait()
            own = G.at[k, 0, c, yl]
            send(("near", k), own, own, near_y)
        elif step == 1:
            arrived("near", k)
            send(("up", k, 1), G.at[k, 0, c], G.at[k, 1, c], up_z)
            send(("dn", k, 1), G.at[k, 0, c], G.at[k, 2, c], dn_z)
            to_mate(k, 0)
        elif step < 4:
            arrived("up", k, step - 1)
            s = 2 * step - 3
            send(("up", k, step), G.at[k, s, c], G.at[k, s + 2, c], up_z)
            arrived("dn", k, step - 1)
            send(("dn", k, step), G.at[k, s + 1, c], G.at[k, s + 3, c], dn_z)
            to_mate(k, step - 1)
        elif step == 4:
            arrived("up", k, 3)
            send(("up", k, 4), G.at[k, 5, c, 0], G.at[k, 7, c, 0], up_z)
            arrived("dn", k, 3)
            send(("dn", k, 4), G.at[k, 6, c, 1], G.at[k, 7, c, 1], dn_z)
            to_mate(k, 3)
        else:
            arrived("up", k, 4)
            arrived("dn", k, 4)
            to_mate(k, 4)

    def up_proj(k, g):
        s, n = GROUPS[g]
        if NC not in waited:
            waited.add(NC)
            loads[NC].wait()
        arrived("mate", k, g)

        @pl.loop(0, 3)
        def _(t):
            cols = pl.ds(pl.multiple_of(t * 256, 256), 256)
            lhs = G[k, pl.ds(s, n)].reshape(n * 4 * RB, 1536)
            r = jnp.dot(lhs, W1[:, cols], preferred_element_type=jnp.float32)
            r = r.reshape(n, 4, RB, 256)
            for i in range(n):
                for j in range(4):
                    XF[k, j, s + i, :, cols] = r[i, j]
                    XS[k, j, s + i, :, cols] = r[i, j].astype(jnp.bfloat16)

        for d in (1, 0, 2):
            send(("xs", k, g, d), XS.at[k, xs[d], pl.ds(s, n)], XR.at[k, d, pl.ds(s, n)], x_dev[d])

    def x_sum(k, g):
        s, n = GROUPS[g]
        for d in range(3):
            arrived("xs", k, g, d)
        rows = pl.ds(s, n)
        total = XF[k, x, rows]
        for d in range(3):
            total = total + XR[k, d, rows].astype(jnp.float32)
        YS[k, rows] = total
        send(("far", k, g), YS.at[k, rows], YR.at[k, rows], far_y)

    def activate(k, g):
        s, n = GROUPS[g]
        arrived("far", k, g)
        rows = pl.ds(s, n)
        v = YS[k, rows] + YR[k, rows] + b1[...].reshape(1, 1, 768)
        A[k, x, rows] = jax.nn.gelu(v, approximate=True).astype(jnp.bfloat16)
        for d in (1, 0, 2):
            send(("act", k, g, d), A.at[k, x, rows], A.at[k, x, rows], x_dev[d])

    def down_proj(k, g):
        s, n = GROUPS[g]
        if NC + 1 not in waited:
            waited.add(NC + 1)
            loads[NC + 1].wait()
        for d in range(3):
            arrived("act", k, g, d)
        first = c == 0

        @pl.loop(0, 6)
        def _(t):
            cols = pl.ds(pl.multiple_of(t * 256, 256), 256)
            lhs = A[k, :, pl.ds(s, n)].reshape(4 * n * RB, 768)
            r = jnp.dot(lhs, W2[:, cols], preferred_element_type=jnp.float32)
            r = r.reshape(2, 2, n, RB, 256)
            mine = jnp.where(first, r[0], r[1])
            other = jnp.where(first, r[1], r[0]).astype(CORE)
            for i in range(n):
                for j in range(2):
                    OF[k, s + i, j, :, cols] = mine[j, i]
                    CS[k, s + i, j, :, cols] = other[j, i]

        send(("core", k, g), CS.at[k, pl.ds(s, n)], CR.at[k, pl.ds(s, n)], mate)

    def reduce_z(k, g):
        s, n = GROUPS[g]
        arrived("core", k, g)

        def term(slot, block):
            return OF[k, slot, block] + CR[k, slot, block].astype(jnp.float32)

        if g == 4:
            for b in range(2):
                ZS[k, 7, b] = term(7, b).astype(jnp.bfloat16)
            send(("zdn", k, 4), ZS.at[k, 7, 0], ZR.at[k, 5, 0], dn_z)
            send(("zup", k, 4), ZS.at[k, 7, 1], ZR.at[k, 6, 1], up_z)
        elif g > 0:
            for name, slot, dev, there in (("zdn", s, dn_z, (s - 2) if g > 1 else 0), ("zup", s + 1, up_z, (s - 1) if g > 1 else 7)):
                arrived(name, k, g + 1)
                for b in range(2):
                    v = term(slot, b)
                    if g < 3 or b == (0 if name == "zdn" else 1):
                        v = v + ZR[k, slot, b].astype(jnp.float32)
                    ZS[k, slot, b] = v.astype(jnp.bfloat16)
                send((name, k, g), ZS.at[k, slot], ZR.at[k, there], dev)
        else:
            arrived("zdn", k, 1)
            arrived("zup", k, 1)
            for b in range(2):
                FS[k, b] = term(0, b) + ZR[k, 0, b].astype(jnp.float32) + ZR[k, 7, b].astype(jnp.float32)
            LS[k] = FS[k, 1 - yl]
            send(("last", k), LS.at[k], LR.at[k], near_y)

    def finish(k):
        arrived("last", k)
        v = FS[k, yl] + LR[k] + b2[...]
        out[pl.ds(k * RB, RB)] = v.astype(jnp.bfloat16)

    what = (gather, up_proj, x_sum, activate, down_proj, reduce_z, finish)
    for w, k, i in ORDER:
        what[w](*((k,) if w == 6 else (k, i)))

    for copy in copies.values():
        copy.wait_send()


def per_device(tokens, up_weight, up_bias, down_weight, down_bias):
    f32, bf16 = jnp.float32, jnp.bfloat16
    any_spec = pl.BlockSpec(memory_space=pl.ANY)
    vmem = pl.BlockSpec(memory_space=pltpu.VMEM)
    n_copies = NC * 64
    return pl.pallas_call(
        kernel,
        out_shape=jax.ShapeDtypeStruct((48, 1536), bf16),
        in_specs=[any_spec, any_spec, vmem, any_spec, vmem],
        out_specs=vmem,
        scratch_shapes=[
            pltpu.VMEM((NC, NZ, 2, 2, RB, 1536), bf16),
            pltpu.VMEM((1536, 768), bf16),
            pltpu.VMEM((768, 1536), bf16),
            pltpu.VMEM((NC, 4, NZ, RB, 768), f32),
            pltpu.VMEM((NC, 4, NZ, RB, 768), bf16),
            pltpu.VMEM((NC, 3, NZ, RB, 768), bf16),
            pltpu.VMEM((NC, NZ, RB, 768), f32),
            pltpu.VMEM((NC, NZ, RB, 768), f32),
            pltpu.VMEM((NC, 4, NZ, RB, 768), bf16),
            pltpu.VMEM((NC, NZ, 2, RB, 1536), f32),
            pltpu.VMEM((NC, NZ, 2, RB, 1536), CORE),
            pltpu.VMEM((NC, NZ, 2, RB, 1536), CORE),
            pltpu.VMEM((NC, NZ, 2, RB, 1536), bf16),
            pltpu.VMEM((NC, NZ, 2, RB, 1536), bf16),
            pltpu.VMEM((NC, 2, RB, 1536), f32),
            pltpu.VMEM((NC, RB, 1536), f32),
            pltpu.VMEM((NC, RB, 1536), f32),
            pltpu.SemaphoreType.DMA((NC + 2,)),
            pltpu.SemaphoreType.DMA((n_copies,)),
            pltpu.SemaphoreType.DMA((n_copies,)),
        ],
        compiler_params=pltpu.CompilerParams(
            collective_id=0, has_side_effects=True, vmem_limit_bytes=56 * 2**20
        ),
        cost_estimate=pl.CostEstimate(flops=7_300_000_000, bytes_accessed=5_000_000, transcendentals=600_000),
    )(tokens, up_weight, up_bias.reshape(1, 768), down_weight, down_bias.reshape(1, 1536))


def solution(mesh):
    return jax.shard_map(
        per_device,
        mesh=mesh,
        in_specs=(
            P(("row", "col"), "depth"),
            P("depth", ("row", "col")),
            P(("row", "col")),
            P(("row", "col"), "depth"),
            P("depth"),
        ),
        out_specs=P(("row", "col"), "depth"),
        check_vma=False,
    )
```
